128 devices in a mesh: outer: 8 (over y_lo, z), inner: 8 (over x, y_hi), head: 2 (over core).
Axes of the slice: x: 4, y: 4 (y_hi: 2, y_lo: 2; y = y_hi * 2 + y_lo), z: 4, core: 2. Of those that a mesh axis runs over, the one named last changes fastest.
Arguments:
- queries: bfloat16 [32768, 4, 8, 128], P(('outer', 'inner'), None, 'head'), may hold values from -6 to 6
- key_heads: bfloat16 [32768, 4, 128], P(('outer', 'inner')), may hold values from -6 to 6
- value_heads: bfloat16 [32768, 4, 128], P(('outer', 'inner')), may hold values from -6 to 6
- outputs: bfloat16 [32768, 4, 8, 128], P(('outer', 'inner'), None, 'head'), may hold values from -6 to 6
- out_grad: bfloat16 [32768, 4, 8, 128], P(('outer', 'inner'), None, 'head'), may hold values from -6 to 6
- log_norm: float32 [4, 8, 32768], P(None, 'head', ('outer', 'inner')), may hold values from 3 to 7
- tree_spans: int32 [3, 32768], P(None, ('outer', 'inner')), may hold values from 0 to 32767, as said below
Outputs:
- query_grad: bfloat16 [32768, 4, 8, 128], P(('outer', 'inner'), None, 'head')
- key_grad: bfloat16 [32768, 4, 128], P(('outer', 'inner'), 'head')
- value_grad: bfloat16 [32768, 4, 128], P(('outer', 'inner'), 'head')
The draws below stay inside these ranges and needn't reach their ends.
Inputs may be any that keep to these rules, and one draw needn't show every extreme that they name: `tree_spans`: the sequence is packed with rollout trees, each a run of tokens with a shared prompt followed by four branches (some may be empty). For a token, row 0 is its tree's first token; row 1 ends the prompt for branch tokens and equals row 0 for prompt tokens; row 2 is the first token of its own branch, or row 0 for prompt tokens. Apart from the first and the last, one tree starts in every third shard of 512 tokens. The last token of the sequence is a branch of its own. A key is visible only to queries of its own shard and the 3 shards after it, and in every draw some key is visible that far.
All inputs are finite; a program needn't handle non-finite values.
Results may differ from the reference program's by a relative error of at most 0.0058.
Values may be sent and summed in bfloat16 or wider, within the bound.
No kernel may reach another device: no remote copies, remote signals or barrier semaphores. Data moves between devices by JAX's collectives and lax.ppermute only.
A program may use at most 256 MiB of HBM per device.

```python
import math
import jax
import jax.numpy as jnp
from jax import lax

KVH = 4
GROUP = 8
HD = 128
REACH = 4
TOK_DEV = 512
TOKENS = 32768


def draw_tree_spans(key, part):
    key = jax.random.fold_in(key, 7)
    shards = TOKENS // TOK_DEV
    tree_count = shards // 3
    first_key, second_key, third_key, fourth_key = jax.random.split(key, 4)
    tree_ids = jnp.arange(tree_count, dtype=jnp.int32)
    offsets = jax.random.randint(first_key, (tree_count,), 2, TOK_DEV, dtype=jnp.int32)
    forced = jax.random.randint(second_key, (), 0, tree_count - 1, dtype=jnp.int32)
    offsets = jnp.where(tree_ids == forced, TOK_DEV - 1, offsets)
    starts = 3 * TOK_DEV * tree_ids + offsets
    bounds = jnp.concatenate([jnp.zeros((1,), jnp.int32), starts, jnp.full((1,), TOKENS, jnp.int32)])
    lengths = bounds[1:] - bounds[:-1]
    prompts = jax.random.randint(third_key, (tree_count + 1,), 1, lengths // 2 + 1, dtype=jnp.int32)
    cut_lower = (bounds[:-1] + prompts)[:, None]
    cut_upper = bounds[1:][:, None]
    cut_points = jax.random.randint(fourth_key, (tree_count + 1, 3), cut_lower, cut_upper, dtype=jnp.int32)
    cut_points = cut_points.at[tree_count, 2].set(TOKENS - 1)
    cut_points = jnp.sort(cut_points, axis=1)
    positions = jnp.arange(TOKENS, dtype=jnp.int32)
    tree_owner = jnp.sum((positions[:, None] >= starts[None, :]).astype(jnp.int32), axis=1)
    tree_start = bounds[tree_owner]
    prompt_end = tree_start + prompts[tree_owner]
    token_cuts = cut_points[tree_owner]
    branch_start = jnp.max(jnp.where(token_cuts <= positions[:, None], token_cuts, prompt_end[:, None]), axis=1)
    in_prompt = positions < prompt_end
    prefix_end = jnp.where(in_prompt, tree_start, prompt_end)
    own_start = jnp.where(in_prompt, tree_start, branch_start)
    return jnp.stack([tree_start, prefix_end, own_start]).astype(jnp.int32)


def level_of(key, dims, cuts, low, largest):
    level = 1.0
    for dim, blocks in cuts:
        heights = jax.random.uniform(jax.random.fold_in(jax.random.fold_in(key, 6), dim), (blocks,), jnp.float32, low / len(cuts), largest / len(cuts))
        level = level * jnp.repeat(jnp.exp(heights), dims[dim] // blocks).reshape((-1,) + (1,) * (len(dims) - 1 - dim))
    return level


def centred(rng, shape, width, limit, cuts=(), kind=jnp.bfloat16):
    loudness = level_of(rng, shape, cuts, -0.22, 0.18) if cuts else 1.0
    values = jax.random.normal(rng, shape, jnp.float32) * width * loudness
    return jnp.minimum(jnp.maximum(values, -limit), limit).astype(kind)


def setup_inputs(seed: int = 0) -> dict:
    key_of = jax.random.split(jax.random.key(seed), 8)
    return {
        "queries": centred(key_of[0], (TOKENS, KVH, GROUP, HD), 1.0, 6.0, ((0, 64), (2, 2))),
        "key_heads": centred(key_of[1], (TOKENS, KVH, HD), 1.0, 6.0, ((0, 64),)),
        "value_heads": centred(key_of[2], (TOKENS, KVH, HD), 1.0, 6.0, ((0, 64),)),
        "outputs": centred(key_of[3], (TOKENS, KVH, GROUP, HD), 1.0, 6.0, ((0, 64), (2, 2))),
        "out_grad": centred(key_of[4], (TOKENS, KVH, GROUP, HD), 1.0, 6.0, ((0, 64), (2, 2))),
        "log_norm": jnp.clip(3.0 + 4.0 * jax.random.uniform(key_of[5], (KVH, GROUP, TOKENS), jnp.float32) ** level_of(key_of[5], (KVH, GROUP, TOKENS), ((1, 2), (2, 64)), -0.2, 0.2), 3.0, 7.0),
        "tree_spans": draw_tree_spans(jax.random.fold_in(key_of[7], 71), 0),
    }


def seen_mask(span_block, query_pos, key_pos):
    keys_col = key_pos[None, :]
    in_prefix = (keys_col >= span_block[0][:, None]) & (keys_col < span_block[1][:, None])
    in_branch = (keys_col >= span_block[2][:, None]) & (keys_col <= query_pos[:, None])
    return in_prefix | in_branch

def reference(queries, key_heads, value_heads, outputs, out_grad, log_norm, tree_spans):
    tokens, kv_heads, group_size, head_size = queries.shape
    score_scale = 1.0 / math.sqrt(head_size)
    lookback = (REACH - 1) * TOK_DEV
    window = REACH * TOK_DEV
    key_padded = jnp.concatenate([jnp.zeros((lookback, kv_heads, head_size), key_heads.dtype), key_heads], axis=0)
    value_padded = jnp.concatenate([jnp.zeros((lookback, kv_heads, head_size), value_heads.dtype), value_heads], axis=0)
    row_delta = jnp.einsum('thgd,thgd->hgt', out_grad.astype(jnp.float32), outputs.astype(jnp.float32))
    offsets = jnp.arange(TOK_DEV, dtype=jnp.int32)
    window_offsets = jnp.arange(window, dtype=jnp.int32)

    def one_block(carried, block_index):
        first_row = (block_index * TOK_DEV).astype(jnp.int32)
        query_block = lax.dynamic_slice_in_dim(queries, first_row, TOK_DEV, 0).astype(jnp.float32)
        grad_block = lax.dynamic_slice_in_dim(out_grad, first_row, TOK_DEV, 0).astype(jnp.float32)
        norm_block = lax.dynamic_slice_in_dim(log_norm, first_row, TOK_DEV, 2)
        delta_block = lax.dynamic_slice_in_dim(row_delta, first_row, TOK_DEV, 2)
        span_block = lax.dynamic_slice_in_dim(tree_spans, first_row, TOK_DEV, 1)
        key_block = lax.dynamic_slice_in_dim(key_padded, first_row, window, 0).astype(jnp.float32)
        value_block = lax.dynamic_slice_in_dim(value_padded, first_row, window, 0).astype(jnp.float32)
        query_pos = first_row + offsets
        key_pos = first_row - lookback + window_offsets
        visible = seen_mask(span_block, query_pos, key_pos)
        scores = jnp.einsum('thgd,khd->hgtk', query_block, key_block) * score_scale
        weights = jnp.where(visible[None, None], jnp.exp(scores - norm_block[:, :, :, None]), 0.0)
        prob_grad = jnp.einsum('thgd,khd->hgtk', grad_block, value_block)
        score_grad = weights * (prob_grad - delta_block[:, :, :, None])
        weight_half = lax.optimization_barrier(weights.astype(jnp.bfloat16)).astype(jnp.float32)
        score_half = lax.optimization_barrier(score_grad.astype(jnp.bfloat16)).astype(jnp.float32)
        value_part = jnp.einsum('hgtk,thgd->khd', weight_half, grad_block)
        key_part = jnp.einsum('hgtk,thgd->khd', score_half, query_block)
        query_part = jnp.einsum('hgtk,khd->thgd', score_half, key_block)
        current = lax.dynamic_slice_in_dim(carried, first_row, window, 1)
        carried = lax.dynamic_update_slice_in_dim(carried, current + jnp.stack([key_part, value_part]), first_row, 1)
        return (carried, (query_part * score_scale).astype(jnp.bfloat16))
    initial = jnp.zeros((2, tokens + lookback, kv_heads, head_size), jnp.float32)
    carried, query_blocks = lax.scan(one_block, initial, jnp.arange(tokens // TOK_DEV, dtype=jnp.int32))
    query_grad = query_blocks.reshape(queries.shape)
    key_grad = (carried[0, lookback:] * score_scale).astype(jnp.bfloat16)
    value_grad = carried[1, lookback:].astype(jnp.bfloat16)
    return (query_grad, key_grad, value_grad)
```

```python
import functools
import math

import jax
import jax.numpy as jnp
from jax import lax
from jax.experimental import pallas as pl
from jax.experimental.pallas import tpu as pltpu
from jax.sharding import PartitionSpec as P

SEQ = ("outer", "inner")
LOG2E = math.log2(math.e)
QB = 512
KB = 256
HIDDEN = -1e30

NN = (((1,), (0,)), ((), ()))
NT = (((1,), (1,)), ((), ()))


def dot(a, b, dims):
    return lax.dot_general(a, b, dims, preferred_element_type=jnp.float32)


def tile_kernel(first, last, scale, flags, base, spans, *refs):
    q_refs, g_refs, norm_refs, delta_refs = refs[0:2], refs[2:4], refs[4:6], refs[6:8]
    k_ref, v_ref = refs[8:10]
    rest = refs[10:]
    if first:
        acc = rest[0:2]
        dk_ref, dv_ref = rest[2:4]
        rest = rest[4:]
        for ref in acc:
            ref[...] = jnp.zeros_like(ref)
    else:
        acc = rest[2:4]
        dk_ref, dv_ref = rest[4:6]
        rest = rest[6:]
        if last:
            dq_refs, rest = rest[0:2], rest[2:]
    dk_sum, dv_sum, bias = rest
    heads, rows = q_refs[0].shape[:2]
    keys = k_ref.shape[1]
    q_tiles = rows // QB
    dk_sum[...] = jnp.zeros_like(dk_sum)
    dv_sum[...] = jnp.zeros_like(dv_sum)

    def tile(q0, k0, masked):
        for h in range(heads):
            kk = k_ref[h, pl.ds(k0, KB), :]
            vv = v_ref[h, pl.ds(k0, KB), :]
            for s in range(2):
                qq = q_refs[s][h, pl.ds(q0, QB), :]
                gg = g_refs[s][h, pl.ds(q0, QB), :]
                score = dot(kk, qq, NT) * (scale * LOG2E) - norm_refs[s][h, :, pl.ds(q0, QB)]
                if masked:
                    score = score + bias[...]
                weight = jnp.exp2(score)
                grad = weight * (dot(vv, gg, NT) - delta_refs[s][h, :, pl.ds(q0, QB)])
                weight = weight.astype(jnp.bfloat16)
                grad = grad.astype(jnp.bfloat16)
                dv_sum[h, pl.ds(k0, KB), :] += dot(weight, gg, NN)
                dk_sum[h, pl.ds(k0, KB), :] += dot(grad, qq, NN)
                acc[s][h, :, pl.ds(q0, QB)] += dot(kk.T, grad, NN)

    def step(index, carry):
        kind = flags[index]
        q0 = pl.multiple_of((index % q_tiles) * QB, QB)
        k0 = pl.multiple_of((index // q_tiles) * KB, KB)

        @pl.when(kind == 1)
        def _():
            key = base[0] + k0 + lax.broadcasted_iota(jnp.int32, (KB, QB), 0)
            low, high, own, pos = [spans[i : i + 1, pl.ds(q0, QB)] for i in range(4)]
            seen = ((key >= low) & (key < high)) | ((key >= own) & (key <= pos))
            bias[...] = jnp.where(seen, 0.0, HIDDEN)
            tile(q0, k0, True)

        @pl.when(kind == 2)
        def _():
            tile(q0, k0, False)

        return carry

    lax.fori_loop(0, q_tiles * (keys // KB), step, 0)
    dk_ref[...] = dk_sum[...].astype(dk_ref.dtype)
    dv_ref[...] = dv_sum[...].astype(dv_ref.dtype)
    if last:
        for s in range(2):
            for h in range(heads):
                for r in range(rows // QB):
                    part = acc[s][h, :, r * QB : (r + 1) * QB] * scale
                    dq_refs[s][h, r * QB : (r + 1) * QB, :] = part.T.astype(jnp.bfloat16)


def tiles(flags, base, spans, q, g, norm, delta, k, v, acc, last, scale, kind):
    heads, rows, size = q[0].shape
    keys = k.shape[1]
    first = acc is None
    vmem = pl.BlockSpec(memory_space=pltpu.VMEM)
    smem = pl.BlockSpec(memory_space=pltpu.SMEM)
    acc_shape = jax.ShapeDtypeStruct((heads, size, rows), jnp.float32)
    part = jax.ShapeDtypeStruct((heads, keys, size), kind)
    operands = [flags, base, spans, *q, *g, *norm, *delta, k, v]
    aliases = {}
    if not first:
        aliases = {len(operands): 0, len(operands) + 1: 1}
        operands += list(acc)
    outs = [acc_shape, acc_shape, part, part]
    if last:
        outs += [jax.ShapeDtypeStruct((heads, rows, size), jnp.bfloat16)] * 2
    return pl.pallas_call(
        functools.partial(tile_kernel, first, last, scale),
        in_specs=[smem, smem] + [vmem] * (len(operands) - 2),
        out_specs=[vmem] * len(outs),
        out_shape=outs,
        scratch_shapes=[
            pltpu.VMEM((heads, keys, size), jnp.float32),
            pltpu.VMEM((heads, keys, size), jnp.float32),
            pltpu.VMEM((KB, QB), jnp.float32),
        ],
        input_output_aliases=aliases,
        compiler_params=pltpu.CompilerParams(vmem_limit_bytes=40 * 2**20),
    )(*operands)


def on_device(shards, queries, key_heads, value_heads, outputs, out_grad, log_norm, tree_spans):
    tokens, kv_heads, group, size = queries.shape
    half = kv_heads // 2
    rows = tokens * group
    scale = 1.0 / math.sqrt(size)
    place = lax.axis_index(SEQ)
    core = lax.axis_index("head")

    def send(block, route):
        pairs = [(s, t) for s, t in route if 0 <= s < shards and 0 <= t < shards]
        return lax.ppermute(block, SEQ, pairs)

    def swap(block):
        return lax.ppermute(block, "head", [(0, 1), (1, 0)])

    def mine(block, axis=0):
        return lax.dynamic_slice_in_dim(block, core * half, half, axis)

    def theirs(block, axis=0):
        return lax.dynamic_slice_in_dim(block, (1 - core) * half, half, axis)

    own_kv = jnp.stack([mine(key_heads, 1), mine(value_heads, 1)]).transpose(0, 2, 1, 3)
    odd = [p % 2 for p in range(shards)]
    to_x = [(p - 2, p) for p in range(shards)]
    to_y = [(p - 3 if odd[p] else p - 1, p) for p in range(shards)]
    to_z = [(p - 1 if odd[p] else p - 3, p) for p in range(shards)]
    kv_x = send(own_kv, to_x)
    kv_z = send(own_kv, to_z)
    kv_y = send(kv_x, [(p ^ 1, p) for p in range(shards)])

    def by_head(block):
        return block.transpose(1, 0, 2, 3).reshape(kv_heads, rows, size)

    q_all, g_all = by_head(queries), by_head(out_grad)
    row_delta = jnp.sum(out_grad.astype(jnp.float32) * outputs.astype(jnp.float32), axis=-1)
    delta_all = row_delta.transpose(1, 0, 2).reshape(kv_heads, 1, rows)
    norm_all = (log_norm * LOG2E).transpose(0, 2, 1).reshape(kv_heads, 1, rows)
    stats = jnp.stack([norm_all, delta_all])
    q_in, g_in = swap(jnp.stack([theirs(q_all), theirs(g_all)]))
    norm_in, delta_in = swap(theirs(stats, 1))
    q = (mine(q_all), q_in)
    g = (mine(g_all), g_in)
    norm = (mine(norm_all), norm_in)
    delta = (mine(delta_all), delta_in)

    pos = place * tokens + jnp.arange(tokens, dtype=jnp.int32)
    odd_here = place % 2
    back = jnp.stack([2 + 0 * place, 1 + 2 * odd_here, 3 - 2 * odd_here, 0 * place])
    bases = (place - back) * tokens
    low_key = bases[:, None] + jnp.arange(tokens // KB, dtype=jnp.int32)[None, :] * KB
    high_key = low_key + KB - 1
    there = ((bases >= 0) & (bases <= place * tokens))[:, None, None]
    lo, hi = low_key[:, :, None], high_key[:, :, None]
    low, high, own = tree_spans[0], tree_spans[1], tree_spans[2]
    some = ((low <= hi) & (high > lo) & (high > low)) | ((own <= hi) & (pos >= lo))
    every = ((low <= lo) & (high > hi)) | ((own <= lo) & (pos >= hi))
    per_tile = (4, tokens // KB, rows // QB, QB // group)
    some = jnp.any((some & there).reshape(per_tile), axis=3)
    every = jnp.all(every.reshape(per_tile), axis=3)
    flags = jnp.where(some, jnp.where(every, 2, 1), 0).astype(jnp.int32).reshape(4, -1)
    spans = jnp.repeat(jnp.concatenate([tree_spans, pos[None]]), group, axis=1)

    def run(which, kv, acc, last, kind=jnp.bfloat16):
        return tiles(
            flags[which], bases[which : which + 1], spans, q, g, norm, delta, kv[0], kv[1],
            acc, last, scale, kind,
        )

    def back_to(route):
        return [(t, s) for s, t in route]

    *acc, dk, dv = run(0, kv_x, None, False)
    from_x = send(jnp.stack([dk, dv]), back_to(to_x))
    *acc, dk, dv = run(2, kv_z, acc, False)
    from_z = send(jnp.stack([dk, dv]), back_to(to_z))
    *acc, dk, dv = run(1, kv_y, acc, False)
    from_y = send(jnp.stack([dk, dv]), back_to(to_y))
    _, _, dk, dv, *dq = run(3, own_kv, acc, True, jnp.float32)

    dq_mine, dq_other = dq[0], swap(dq[1])
    dq_all = jnp.where(
        core == 0, jnp.concatenate([dq_mine, dq_other]), jnp.concatenate([dq_other, dq_mine])
    )
    query_grad = dq_all.reshape(kv_heads, tokens, group, size).transpose(1, 0, 2, 3)

    def total(i, own_part):
        parts = from_x[i].astype(jnp.float32) + from_y[i] + from_z[i] + own_part
        return parts.transpose(1, 0, 2)

    key_grad = (total(0, dk) * scale).astype(jnp.bfloat16)
    value_grad = total(1, dv).astype(jnp.bfloat16)
    return (query_grad, key_grad, value_grad)


def solution(mesh):
    shards = mesh.shape["outer"] * mesh.shape["inner"]
    placed = (
        P(SEQ, None, "head", None),
        P(SEQ, None, None),
        P(SEQ, None, None),
        P(SEQ, None, "head", None),
        P(SEQ, None, "head", None),
        P(None, "head", SEQ),
        P(None, SEQ),
    )
    return jax.shard_map(
        functools.partial(on_device, shards),
        mesh=mesh,
        in_specs=placed,
        out_specs=(P(SEQ, None, "head", None), P(SEQ, "head", None), P(SEQ, "head", None)),
        check_vma=False,
    )
```

```python
import functools
import math

import jax
import jax.numpy as jnp
from jax import lax
from jax.experimental import pallas as pl
from jax.experimental.pallas import tpu as pltpu
from jax.sharding import PartitionSpec as P

SEQ = ("outer", "inner")
LOG2E = math.log2(math.e)
QB = 512
KB = 256
HIDDEN = -1e30

NN = (((1,), (0,)), ((), ()))
NT = (((1,), (1,)), ((), ()))


def dot(a, b, dims):
    return lax.dot_general(a, b, dims, preferred_element_type=jnp.float32)


def tile_kernel(which, first, passing, scale, table, spans, *refs):
    q_refs, g_refs, norm_refs, delta_refs = refs[0:2], refs[2:4], refs[4:6], refs[6:8]
    kv_ref, refs = refs[8], refs[9:]
    if passing:
        pass_in, refs = refs[0], refs[1:]
    rest = refs if first else refs[2:]
    acc, out_ref, rest = rest[0:2], rest[2], rest[3:]
    if passing:
        rest[0][...] = pass_in[...].astype(jnp.float32)
        rest = rest[1:]
    if first:
        for ref in acc:
            ref[...] = jnp.zeros_like(ref)
    dk_sum, dv_sum, bias = rest
    heads, rows = q_refs[0].shape[:2]
    keys = kv_ref.shape[2]
    q_tiles = rows // QB
    dk_sum[...] = jnp.zeros_like(dk_sum)
    dv_sum[...] = jnp.zeros_like(dv_sum)

    def tile(q0, k0, masked):
        for h in range(heads):
            kk = kv_ref[0, h, pl.ds(k0, KB), :]
            vv = kv_ref[1, h, pl.ds(k0, KB), :]
            for s in range(2):
                qq = q_refs[s][h, pl.ds(q0, QB), :]
                gg = g_refs[s][h, pl.ds(q0, QB), :]
                score = dot(kk, qq, NT) * (scale * LOG2E) - norm_refs[s][h, :, pl.ds(q0, QB)]
                if masked:
                    score = score + bias[...]
                weight = jnp.exp2(score)
                grad = weight * (dot(vv, gg, NT) - delta_refs[s][h, :, pl.ds(q0, QB)])
                weight = weight.astype(jnp.bfloat16)
                grad = grad.astype(jnp.bfloat16)
                dv_sum[h, pl.ds(k0, KB), :] += dot(weight, gg, NN)
                dk_sum[h, pl.ds(k0, KB), :] += dot(grad, qq, NN)
                acc[s][h, :, pl.ds(q0, QB)] += dot(kk.T, grad, NN)

    def step(index, carry):
        kind = table[which, 1 + index]
        q0 = pl.multiple_of((index % q_tiles) * QB, QB)
        k0 = pl.multiple_of((index // q_tiles) * KB, KB)

        @pl.when(kind == 1)
        def _():
            key = table[which, 0] + k0 + lax.broadcasted_iota(jnp.int32, (KB, QB), 0)
            low, high, own, pos = [spans[i : i + 1, pl.ds(q0, QB)] for i in range(4)]
            seen = ((key >= low) & (key < high)) | ((key >= own) & (key <= pos))
            bias[...] = jnp.where(seen, 0.0, HIDDEN)
            tile(q0, k0, True)

        @pl.when(kind == 2)
        def _():
            tile(q0, k0, False)

        return carry

    lax.fori_loop(0, q_tiles * (keys // KB), step, 0)
    out_ref[0] = dk_sum[...].astype(out_ref.dtype)
    out_ref[1] = dv_sum[...].astype(out_ref.dtype)


def tiles(which, table, spans, q, g, norm, delta, kv, acc, scale, kind, passed):
    heads, rows, size = q[0].shape
    keys = kv.shape[2]
    vmem = pl.BlockSpec(memory_space=pltpu.VMEM)
    smem = pl.BlockSpec(memory_space=pltpu.SMEM)
    acc_shape = jax.ShapeDtypeStruct((heads, size, rows), jnp.float32)
    part = jax.ShapeDtypeStruct((2, heads, keys, size), kind)
    operands = [table, spans, *q, *g, *norm, *delta, kv]
    outs = [acc_shape, acc_shape, part]
    if passed is not None:
        operands.append(passed)
        outs.append(jax.ShapeDtypeStruct(passed.shape, jnp.float32))
    aliases = {}
    if acc is not None:
        aliases = {len(operands): 0, len(operands) + 1: 1}
        operands += list(acc)
    return pl.pallas_call(
        functools.partial(tile_kernel, which, acc is None, passed is not None, scale),
        in_specs=[smem] + [vmem] * (len(operands) - 1),
        out_specs=[vmem] * len(outs),
        out_shape=outs,
        scratch_shapes=[
            pltpu.VMEM((heads, keys, size), jnp.float32),
            pltpu.VMEM((heads, keys, size), jnp.float32),
            pltpu.VMEM((KB, QB), jnp.float32),
        ],
        input_output_aliases=aliases,
        compiler_params=pltpu.CompilerParams(vmem_limit_bytes=20 * 2**20),
        cost_estimate=pl.CostEstimate(
            flops=20 * heads * 2 * rows * keys * size,
            bytes_accessed=16 * heads * rows * size,
            transcendentals=0,
        ),
    )(*operands)


def round_kernel(scale, acc_own, acc_other, x_ref, z_ref, part_ref, own_ref, *refs):
    other_refs, sum_ref = refs[:-1], refs[-1]
    for h in range(acc_own.shape[0]):
        for r, other_ref in enumerate(other_refs):
            rows = slice(r * QB, (r + 1) * QB)
            own_ref[h, rows, :] = (acc_own[h, :, rows] * scale).T.astype(jnp.bfloat16)
            other_ref[h] = (acc_other[h, :, rows] * scale).T.astype(jnp.bfloat16)
    sum_ref[...] = part_ref[...] + x_ref[...].astype(jnp.float32) + z_ref[...].astype(jnp.float32)


def round_up(acc, from_x, from_z, part, scale):
    heads, size, rows = acc[0].shape
    vmem = pl.BlockSpec(memory_space=pltpu.VMEM)
    shape = jax.ShapeDtypeStruct
    outs = [shape((heads, rows, size), jnp.bfloat16)]
    outs += [shape((heads, QB, size), jnp.bfloat16)] * (rows // QB)
    outs += [shape(part.shape, jnp.float32)]
    return pl.pallas_call(
        functools.partial(round_kernel, scale),
        in_specs=[vmem] * 5,
        out_specs=[vmem] * len(outs),
        out_shape=outs,
        compiler_params=pltpu.CompilerParams(vmem_limit_bytes=20 * 2**20),
        cost_estimate=pl.CostEstimate(
            flops=1, bytes_accessed=12 * heads * rows * size, transcendentals=0
        ),
    )(*acc, from_x, from_z, part)


def finish_kernel(scale, sum_ref, more_ref, key_ref, value_ref):
    for i, (out_ref, factor) in enumerate(((key_ref, scale), (value_ref, 1.0))):
        heads = [
            (sum_ref[i, h] + more_ref[i, h].astype(jnp.float32)) * factor
            for h in range(sum_ref.shape[1])
        ]
        out_ref[...] = jnp.stack(heads, axis=1).astype(out_ref.dtype)


def finish(total, more, scale):
    _, heads, keys, size = total.shape
    vmem = pl.BlockSpec(memory_space=pltpu.VMEM)
    return pl.pallas_call(
        functools.partial(finish_kernel, scale),
        in_specs=[vmem] * 2,
        out_specs=[vmem] * 2,
        out_shape=[jax.ShapeDtypeStruct((keys, heads, size), jnp.bfloat16)] * 2,
        cost_estimate=pl.CostEstimate(
            flops=1, bytes_accessed=8 * heads * keys * size, transcendentals=0
        ),
    )(total, more)


def repeat_lanes(block, repeat):
    size = block.shape[1]
    row = lax.broadcasted_iota(jnp.int32, (size, size * repeat), 0)
    lane = lax.broadcasted_iota(jnp.int32, (size, size * repeat), 1)
    return dot(block, (lane // repeat == row).astype(jnp.bfloat16), NN)


def parts_of(value, count):
    parts = []
    for _ in range(count):
        parts.append(value.astype(jnp.bfloat16))
        value = value - parts[-1].astype(jnp.float32)
    return parts


def prepare_kernel(here, q_hbm, g_hbm, o_hbm, norm_ref, spans_ref, *refs):
    q_own, g_own, q_sent, g_sent, norm_own, delta_own, stats_sent, spans_out = refs[:8]
    buffers, sems = refs[8:11], refs[11]
    tokens, kv_heads, group, size = q_hbm.shape
    half, part = kv_heads // 2, QB // group
    core = here[0]
    copies = []
    for t in range(tokens // part):
        some = pl.ds(t * part, part)
        copies.append(
            [
                pltpu.make_async_copy(hbm.at[some], buffer.at[some], sems.at[i, t])
                for i, (hbm, buffer) in enumerate(zip((q_hbm, g_hbm, o_hbm), buffers))
            ]
        )
        for copy in copies[-1]:
            copy.start()
    lane = lax.broadcasted_iota(jnp.int32, (1, QB), 1)
    ones = jnp.ones((8, size), jnp.bfloat16)
    for t in range(tokens // part):
        for copy in copies[t]:
            copy.wait()
        some, rows = pl.ds(t * part, part), pl.ds(t * QB, QB)
        for j in range(half):
            for other in range(2):
                h = core * half + j if other == 0 else (1 - core) * half + j
                qq, gg, oo = [buffer[some, h].reshape(QB, size) for buffer in buffers]
                terms = parts_of(gg.astype(jnp.float32) * oo.astype(jnp.float32), 2)
                delta = (dot(ones, terms[0], NT) + dot(ones, terms[1], NT))[0:1]
                norm = 0.0
                for piece in parts_of(norm_ref[h, :, some] * LOG2E, 3):
                    wide = repeat_lanes(jnp.concatenate([piece, piece], 0), group)
                    for i in range(group):
                        norm = norm + jnp.where(lane % group == i, wide[i : i + 1], 0.0)
                if other == 0:
                    q_own[j, rows, :], g_own[j, rows, :] = qq, gg
                    norm_own[j, :, rows], delta_own[j, :, rows] = norm, delta
                else:
                    q_sent[j, rows, :], g_sent[j, rows, :] = qq, gg
                    stats_sent[0, j, :, rows], stats_sent[1, j, :, rows] = norm, delta
        spans = spans_ref[:, some]
        pair = jnp.concatenate([spans // 256, spans % 256], 0).astype(jnp.float32)
        wide = repeat_lanes(pair.astype(jnp.bfloat16), group)
        whole = (wide[0:3] * 256.0 + wide[3:6]).astype(jnp.int32)
        spans_out[0:3, rows] = whole
        spans_out[3:4, rows] = here[1] + t * part + lane // group


def prepare(here, queries, out_grad, outputs, log_norm, tree_spans):
    tokens, kv_heads, group, size = queries.shape
    half, rows, bf16 = kv_heads // 2, tokens * group, jnp.bfloat16
    shape = jax.ShapeDtypeStruct
    smem = pl.BlockSpec(memory_space=pltpu.SMEM)
    vmem = pl.BlockSpec(memory_space=pltpu.VMEM)
    hbm = pl.BlockSpec(memory_space=pltpu.HBM)
    return pl.pallas_call(
        prepare_kernel,
        in_specs=[smem, hbm, hbm, hbm, vmem, vmem],
        out_specs=[vmem] * 8,
        out_shape=[shape((half, rows, size), bf16)] * 4
        + [shape((half, 1, rows), jnp.float32)] * 2
        + [shape((2, half, 1, rows), jnp.float32), shape((4, rows), jnp.int32)],
        scratch_shapes=[pltpu.VMEM(queries.shape, bf16)] * 3
        + [pltpu.SemaphoreType.DMA((3, tokens * group // QB))],
        compiler_params=pltpu.CompilerParams(vmem_limit_bytes=48 * 2**20),
        cost_estimate=pl.CostEstimate(
            flops=1, bytes_accessed=10 * kv_heads * rows * size, transcendentals=0
        ),
    )(here, queries, out_grad, outputs, log_norm, tree_spans)


def gather_kernel(here, own_ref, *refs):
    out_ref = refs[-1]
    tokens, kv_heads, group, size = out_ref.shape
    half = kv_heads // 2
    part = QB // group
    for r, other_ref in enumerate(refs[:-1]):
        for j in range(half):
            for h, rows in (
                (here[0] * half + j, own_ref[j, r * QB : (r + 1) * QB, :]),
                ((1 - here[0]) * half + j, other_ref[j]),
            ):
                out_ref[r * part : (r + 1) * part, h] = rows.reshape(part, group, size)


def gather_heads(here, own, others, group):
    half, rows, size = own.shape
    vmem = pl.BlockSpec(memory_space=pltpu.VMEM)
    return pl.pallas_call(
        gather_kernel,
        in_specs=[pl.BlockSpec(memory_space=pltpu.SMEM)] + [vmem] * (1 + len(others)),
        out_specs=vmem,
        out_shape=jax.ShapeDtypeStruct((rows // group, 2 * half, group, size), own.dtype),
        compiler_params=pltpu.CompilerParams(vmem_limit_bytes=20 * 2**20),
        cost_estimate=pl.CostEstimate(
            flops=1, bytes_accessed=8 * half * rows * size, transcendentals=0
        ),
    )(here, own, *others)


def on_device(shards, queries, key_heads, value_heads, outputs, out_grad, log_norm, tree_spans):
    tokens, kv_heads, group, size = queries.shape
    half = kv_heads // 2
    rows = tokens * group
    scale = 1.0 / math.sqrt(size)
    place = lax.axis_index(SEQ)
    core = lax.axis_index("head")

    def send(block, route):
        pairs = [(s, t) for s, t in route if 0 <= s < shards and 0 <= t < shards]
        return lax.ppermute(block, SEQ, pairs)

    def swap(block):
        return lax.ppermute(block, "head", [(0, 1), (1, 0)])

    def mine(block, axis=0):
        return lax.dynamic_slice_in_dim(block, core * half, half, axis)

    own_kv = jnp.stack([mine(key_heads, 1), mine(value_heads, 1)]).transpose(0, 2, 1, 3)
    def ahead_by(block, distance):
        return send(block, [(p, p + distance) for p in range(shards)])

    def back_by(block, distance):
        return send(block, [(p, p - distance) for p in range(shards)])

    kv_1 = ahead_by(own_kv, 1)
    kv_3 = ahead_by(kv_1, 2)
    here = jnp.stack([core, place * tokens]).astype(jnp.int32)
    q_own, g_own, sent_q, sent_g, norm_own, delta_own, stats, spans = prepare(
        here, queries, out_grad, outputs, log_norm, tree_spans
    )
    q_in, g_in = swap(sent_q), swap(sent_g)
    norm_in, delta_in = swap(stats)
    later_kv, spans = lax.optimization_barrier((own_kv, spans))
    kv_2 = ahead_by(later_kv, 2)
    q, g = (q_own, q_in), (g_own, g_in)
    norm, delta = (norm_own, norm_in), (delta_own, delta_in)

    pos = place * tokens + jnp.arange(tokens, dtype=jnp.int32)
    back = jnp.array([1, 2, 3, 0], jnp.int32)
    bases = (place - back) * tokens
    low_key = bases[:, None] + jnp.arange(tokens // KB, dtype=jnp.int32)[None, :] * KB
    high_key = low_key + KB - 1
    there = ((bases >= 0) & (bases <= place * tokens))[:, None, None]
    lo, hi = low_key[:, :, None], high_key[:, :, None]
    low, high, own = tree_spans[0], tree_spans[1], tree_spans[2]
    some = ((low <= hi) & (high > lo) & (high > low)) | ((own <= hi) & (pos >= lo))
    every = ((low <= lo) & (high > hi)) | ((own <= lo) & (pos >= hi))
    per_tile = (4, tokens // KB, rows // QB, QB // group)
    some = jnp.any((some & there).reshape(per_tile), axis=3)
    every = jnp.all(every.reshape(per_tile), axis=3)
    flags = jnp.where(some, jnp.where(every, 2, 1), 0).astype(jnp.int32).reshape(4, -1)
    table = jnp.concatenate([bases[:, None], flags], axis=1)

    def run(which, kv, acc, kind=jnp.bfloat16, passed=None):
        return tiles(which, table, spans, q, g, norm, delta, kv, acc, scale, kind, passed)

    *acc, part = run(0, kv_1, None)
    from_1 = back_by(part, 1)
    *acc, part = run(1, kv_2, acc)
    from_2 = back_by(part, 2)
    *acc, part, kept = run(2, kv_3, acc, passed=from_1)
    from_3 = back_by(part, 3)
    *acc, part = run(3, own_kv, acc, jnp.float32)
    dq_own, *dq_other, total = round_up(acc, kept, from_2, part, scale)
    query_grad = gather_heads(here, dq_own, [swap(block) for block in dq_other], group)
    key_grad, value_grad = finish(total, from_3, scale)
    return (query_grad, key_grad, value_grad)


def solution(mesh):
    shards = mesh.shape["outer"] * mesh.shape["inner"]
    placed = (
        P(SEQ, None, "head", None),
        P(SEQ, None, None),
        P(SEQ, None, None),
        P(SEQ, None, "head", None),
        P(SEQ, None, "head", None),
        P(None, "head", SEQ),
        P(None, SEQ),
    )
    return jax.shard_map(
        functools.partial(on_device, shards),
        mesh=mesh,
        in_specs=placed,
        out_specs=(P(SEQ, None, "head", None), P(SEQ, "head", None), P(SEQ, "head", None)),
        check_vma=False,
    )
```

```python
import functools
import math

import jax
import jax.numpy as jnp
from jax import lax
from jax.experimental import pallas as pl
from jax.experimental.pallas import tpu as pltpu
from jax.sharding import PartitionSpec as P

SEQ = ("outer", "inner")
LOG2E = math.log2(math.e)
QB = 512
KB = 256
HIDDEN = -1e30

NN = (((1,), (0,)), ((), ()))
NT = (((1,), (1,)), ((), ()))


def dot(a, b, dims):
    return lax.dot_general(a, b, dims, preferred_element_type=jnp.float32)


def tile_kernel(which, first, passing, scale, table, spans, *refs):
    q_refs, g_refs, norm_refs, delta_refs = refs[0:2], refs[2:4], refs[4:6], refs[6:8]
    kv_ref, refs = refs[8], refs[9:]
    if passing:
        pass_in, refs = refs[0], refs[1:]
    rest = refs if first else refs[2:]
    acc, out_ref, rest = rest[0:2], rest[2], rest[3:]
    if passing:
        rest[0][...] = pass_in[...].astype(jnp.float32)
        rest = rest[1:]
    if first:
        for ref in acc:
            ref[...] = jnp.zeros_like(ref)
    dk_sum, dv_sum, bias = rest
    heads, rows = q_refs[0].shape[:2]
    keys = kv_ref.shape[2]
    q_tiles = rows // QB
    dk_sum[...] = jnp.zeros_like(dk_sum)
    dv_sum[...] = jnp.zeros_like(dv_sum)

    def tile(q0, k0, width, masked):
        for h in range(heads):
            kk = kv_ref[0, h, pl.ds(k0, width), :]
            vv = kv_ref[1, h, pl.ds(k0, width), :]
            for s in range(2):
                qq = q_refs[s][h, pl.ds(q0, QB), :]
                gg = g_refs[s][h, pl.ds(q0, QB), :]
                score = dot(kk, qq, NT) * (scale * LOG2E) - norm_refs[s][h, :, pl.ds(q0, QB)]
                if masked:
                    score = score + bias[0:width, :]
                weight = jnp.exp2(score)
                grad = weight * (dot(vv, gg, NT) - delta_refs[s][h, :, pl.ds(q0, QB)])
                weight = weight.astype(jnp.bfloat16)
                grad = grad.astype(jnp.bfloat16)
                dv_sum[h, pl.ds(k0, width), :] += dot(weight, gg, NN)
                dk_sum[h, pl.ds(k0, width), :] += dot(grad, qq, NN)
                acc[s][h, :, pl.ds(q0, QB)] += dot(kk.T, grad, NN)

    def step(index, carry):
        kind = table[which, 1 + index]
        q0 = pl.multiple_of((index % q_tiles) * QB, QB)
        k0 = pl.multiple_of((index // q_tiles) * KB, KB)

        def hide(k0, width):
            key = table[which, 0] + k0 + lax.broadcasted_iota(jnp.int32, (width, QB), 0)
            low, high, own, pos = [spans[i : i + 1, pl.ds(q0, QB)] for i in range(4)]
            seen = ((key >= low) & (key < high)) | ((key >= own) & (key <= pos))
            bias[0:width, :] = jnp.where(seen, 0.0, HIDDEN)

        @pl.when(kind == 3)
        def _():
            hide(k0, KB)
            tile(q0, k0, KB, True)

        @pl.when(kind == 4)
        def _():
            tile(q0, k0, KB, False)

        @pl.when((kind == 1) | (kind == 2))
        def _():
            part = pl.multiple_of(k0 + (kind - 1) * (KB // 2), KB // 2)
            hide(part, KB // 2)
            tile(q0, part, KB // 2, True)

        return carry

    lax.fori_loop(0, q_tiles * (keys // KB), step, 0)
    out_ref[0] = dk_sum[...].astype(out_ref.dtype)
    out_ref[1] = dv_sum[...].astype(out_ref.dtype)


def tiles(which, table, spans, q, g, norm, delta, kv, acc, scale, kind, passed):
    heads, rows, size = q[0].shape
    keys = kv.shape[2]
    vmem = pl.BlockSpec(memory_space=pltpu.VMEM)
    smem = pl.BlockSpec(memory_space=pltpu.SMEM)
    acc_shape = jax.ShapeDtypeStruct((heads, size, rows), jnp.float32)
    part = jax.ShapeDtypeStruct((2, heads, keys, size), kind)
    operands = [table, spans, *q, *g, *norm, *delta, kv]
    outs = [acc_shape, acc_shape, part]
    if passed is not None:
        operands.append(passed)
        outs.append(jax.ShapeDtypeStruct(passed.shape, jnp.float32))
    aliases = {}
    if acc is not None:
        aliases = {len(operands): 0, len(operands) + 1: 1}
        operands += list(acc)
    return pl.pallas_call(
        functools.partial(tile_kernel, which, acc is None, passed is not None, scale),
        in_specs=[smem] + [vmem] * (len(operands) - 1),
        out_specs=[vmem] * len(outs),
        out_shape=outs,
        scratch_shapes=[
            pltpu.VMEM((heads, keys, size), jnp.float32),
            pltpu.VMEM((heads, keys, size), jnp.float32),
            pltpu.VMEM((KB, QB), jnp.float32),
        ],
        input_output_aliases=aliases,
        compiler_params=pltpu.CompilerParams(vmem_limit_bytes=20 * 2**20),
        cost_estimate=pl.CostEstimate(
            flops=20 * heads * 2 * rows * keys * size,
            bytes_accessed=16 * heads * rows * size,
            transcendentals=0,
        ),
    )(*operands)


def round_kernel(scale, acc_own, acc_other, own_ref, *other_refs):
    for h in range(acc_own.shape[0]):
        for r, other_ref in enumerate(other_refs):
            rows = slice(r * QB, (r + 1) * QB)
            own_ref[h, rows, :] = (acc_own[h, :, rows] * scale).T.astype(jnp.bfloat16)
            other_ref[h] = (acc_other[h, :, rows] * scale).T.astype(jnp.bfloat16)


def round_up(acc, scale):
    heads, size, rows = acc[0].shape
    vmem = pl.BlockSpec(memory_space=pltpu.VMEM)
    shape = jax.ShapeDtypeStruct
    outs = [shape((heads, rows, size), jnp.bfloat16)]
    outs += [shape((heads, QB, size), jnp.bfloat16)] * (rows // QB)
    return pl.pallas_call(
        functools.partial(round_kernel, scale),
        in_specs=[vmem] * 2,
        out_specs=[vmem] * len(outs),
        out_shape=outs,
        compiler_params=pltpu.CompilerParams(vmem_limit_bytes=20 * 2**20),
        cost_estimate=pl.CostEstimate(
            flops=1, bytes_accessed=12 * heads * rows * size, transcendentals=0
        ),
    )(*acc)


def finish_kernel(scale, sum_ref, more_ref, key_ref, value_ref, rows_ref):
    heads, keys, size = sum_ref.shape[1:]
    for i, (out_ref, factor) in enumerate(((key_ref, scale), (value_ref, 1.0))):
        for h in range(heads):
            rows_ref[i, pl.ds(h, keys, stride=heads), :] = (
                sum_ref[i, h] + more_ref[i, h].astype(jnp.float32)
            ) * factor
        out_ref[...] = rows_ref[i].astype(out_ref.dtype).reshape(keys, heads, size)


def finish(total, more, scale):
    _, heads, keys, size = total.shape
    vmem = pl.BlockSpec(memory_space=pltpu.VMEM)
    return pl.pallas_call(
        functools.partial(finish_kernel, scale),
        in_specs=[vmem] * 2,
        out_specs=[vmem] * 2,
        out_shape=[jax.ShapeDtypeStruct((keys, heads, size), jnp.bfloat16)] * 2,
        scratch_shapes=[pltpu.VMEM((2, keys * heads, size), jnp.float32)],
        cost_estimate=pl.CostEstimate(
            flops=1, bytes_accessed=8 * heads * keys * size, transcendentals=0
        ),
    )(in_vmem(total), in_vmem(more))


def in_vmem(array):
    return pltpu.with_memory_space_constraint(array, pltpu.VMEM)


def repeat_lanes(block, repeat):
    size = block.shape[1]
    row = lax.broadcasted_iota(jnp.int32, (size, size * repeat), 0)
    lane = lax.broadcasted_iota(jnp.int32, (size, size * repeat), 1)
    return dot(block, (lane // repeat == row).astype(jnp.bfloat16), NN)


def parts_of(value, count):
    parts = []
    for _ in range(count):
        parts.append(value.astype(jnp.bfloat16))
        value = value - parts[-1].astype(jnp.float32)
    return parts


def prepare_kernel(here, q_hbm, g_hbm, o_hbm, norm_ref, spans_ref, *refs):
    q_own, g_own, q_sent, g_sent, norm_own, delta_own, stats_sent, spans_out = refs[:8]
    buffers, sems = refs[8:11], refs[11]
    tokens, kv_heads, group, size = q_hbm.shape
    half, part = kv_heads // 2, QB // group
    core = here[0]
    copies = []
    for t in range(tokens // part):
        some = pl.ds(t * part, part)
        copies.append(
            [
                pltpu.make_async_copy(hbm.at[some], buffer.at[some], sems.at[i, t])
                for i, (hbm, buffer) in enumerate(zip((q_hbm, g_hbm, o_hbm), buffers))
            ]
        )
        for copy in copies[-1]:
            copy.start()
    lane = lax.broadcasted_iota(jnp.int32, (1, QB), 1)
    ones = jnp.ones((8, size), jnp.bfloat16)
    for t in range(tokens // part):
        for copy in copies[t]:
            copy.wait()
        some, rows = pl.ds(t * part, part), pl.ds(t * QB, QB)
        for j in range(half):
            for other in range(2):
                h = core * half + j if other == 0 else (1 - core) * half + j
                qq, gg, oo = [buffer[some, h].reshape(QB, size) for buffer in buffers]
                terms = parts_of(gg.astype(jnp.float32) * oo.astype(jnp.float32), 2)
                delta = (dot(ones, terms[0], NT) + dot(ones, terms[1], NT))[0:1]
                norm = 0.0
                for piece in parts_of(norm_ref[h, :, some] * LOG2E, 3):
                    wide = repeat_lanes(jnp.concatenate([piece, piece], 0), group)
                    for i in range(group):
                        norm = norm + jnp.where(lane % group == i, wide[i : i + 1], 0.0)
                if other == 0:
                    q_own[j, rows, :], g_own[j, rows, :] = qq, gg
                    norm_own[j, :, rows], delta_own[j, :, rows] = norm, delta
                else:
                    q_sent[j, rows, :], g_sent[j, rows, :] = qq, gg
                    stats_sent[0, j, :, rows], stats_sent[1, j, :, rows] = norm, delta
        spans = spans_ref[:, some]
        pair = jnp.concatenate([spans // 256, spans % 256], 0).astype(jnp.float32)
        wide = repeat_lanes(pair.astype(jnp.bfloat16), group)
        whole = (wide[0:3] * 256.0 + wide[3:6]).astype(jnp.int32)
        spans_out[0:3, rows] = whole
        spans_out[3:4, rows] = here[1] + t * part + lane // group


def prepare(here, queries, out_grad, outputs, log_norm, tree_spans):
    tokens, kv_heads, group, size = queries.shape
    half, rows, bf16 = kv_heads // 2, tokens * group, jnp.bfloat16
    shape = jax.ShapeDtypeStruct
    smem = pl.BlockSpec(memory_space=pltpu.SMEM)
    vmem = pl.BlockSpec(memory_space=pltpu.VMEM)
    hbm = pl.BlockSpec(memory_space=pltpu.HBM)
    pinned = [
        pltpu.with_memory_space_constraint(array, pltpu.HBM)
        for array in (queries, out_grad, outputs)
    ]
    return pl.pallas_call(
        prepare_kernel,
        in_specs=[smem, hbm, hbm, hbm, vmem, vmem],
        out_specs=[vmem] * 8,
        out_shape=[pltpu.VMEM((half, rows, size), bf16)] * 2
        + [shape((half, rows, size), bf16)] * 2
        + [shape((half, 1, rows), jnp.float32)] * 2
        + [shape((2, half, 1, rows), jnp.float32), shape((4, rows), jnp.int32)],
        scratch_shapes=[pltpu.VMEM(queries.shape, bf16)] * 3
        + [pltpu.SemaphoreType.DMA((3, tokens * group // QB))],
        compiler_params=pltpu.CompilerParams(vmem_limit_bytes=48 * 2**20),
        cost_estimate=pl.CostEstimate(
            flops=1, bytes_accessed=10 * kv_heads * rows * size, transcendentals=0
        ),
    )(here, *pinned, log_norm, tree_spans)


def gather_kernel(here, own_ref, *refs):
    others, (part_ref, kept_ref, more_ref, rows_ref, sum_ref) = refs[:-5], refs[-5:]
    _, kv_heads, group, size = rows_ref.shape
    half = kv_heads // 2
    part = QB // group
    for r, other_ref in enumerate(others):
        some = pl.ds(r * part, part)
        for j in range(half):
            for h, rows in (
                (here[0] * half + j, own_ref[j, r * QB : (r + 1) * QB, :]),
                ((1 - here[0]) * half + j, other_ref[j]),
            ):
                rows_ref[some, h] = rows.reshape(part, group, size)
    sum_ref[...] = part_ref[...] + kept_ref[...] + more_ref[...].astype(jnp.float32)


def gather_heads(here, own, others, group, terms):
    half, rows, size = own.shape
    vmem = pl.BlockSpec(memory_space=pltpu.VMEM)
    shape = (rows // group, 2 * half, group, size)
    return pl.pallas_call(
        gather_kernel,
        in_specs=[pl.BlockSpec(memory_space=pltpu.SMEM)] + [vmem] * (1 + len(others) + len(terms)),
        out_specs=[vmem, vmem],
        out_shape=[
            jax.ShapeDtypeStruct(shape, own.dtype),
            jax.ShapeDtypeStruct(terms[0].shape, jnp.float32),
        ],
        compiler_params=pltpu.CompilerParams(vmem_limit_bytes=20 * 2**20),
        cost_estimate=pl.CostEstimate(
            flops=1, bytes_accessed=8 * half * rows * size, transcendentals=0
        ),
    )(here, own, *others, *terms)


def on_device(shards, queries, key_heads, value_heads, outputs, out_grad, log_norm, tree_spans):
    tokens, kv_heads, group, size = queries.shape
    half = kv_heads // 2
    rows = tokens * group
    scale = 1.0 / math.sqrt(size)
    place = lax.axis_index(SEQ)
    core = lax.axis_index("head")

    def send(block, route):
        pairs = [(s, t) for s, t in route if 0 <= s < shards and 0 <= t < shards]
        return lax.ppermute(block, SEQ, pairs)

    def swap(block):
        return lax.ppermute(block, "head", [(0, 1), (1, 0)])

    def mine(block, axis=0):
        return lax.dynamic_slice_in_dim(block, core * half, half, axis)

    own_kv = jnp.stack([mine(key_heads, 1), mine(value_heads, 1)]).transpose(0, 2, 1, 3)
    def ahead_by(block, distance):
        return send(block, [(p, p + distance) for p in range(shards)])

    def back_by(block, distance):
        return send(block, [(p, p - distance) for p in range(shards)])

    kv_1 = ahead_by(own_kv, 1)
    kv_3 = ahead_by(kv_1, 2)
    here = jnp.stack([core, place * tokens]).astype(jnp.int32)
    q_own, g_own, sent_q, sent_g, norm_own, delta_own, stats, spans = prepare(
        here, queries, out_grad, outputs, log_norm, tree_spans
    )
    q_in, g_in = swap(sent_q), swap(sent_g)
    norm_in, delta_in = swap(stats)
    later_kv, spans = lax.optimization_barrier((own_kv, spans))
    kv_2 = ahead_by(later_kv, 2)
    q, g = (q_own, q_in), (g_own, g_in)
    norm, delta = (norm_own, norm_in), (delta_own, delta_in)

    pos = place * tokens + jnp.arange(tokens, dtype=jnp.int32)
    back = jnp.array([1, 2, 3, 0], jnp.int32)
    bases = (place - back) * tokens
    width = KB // 2
    low_key = bases[:, None] + jnp.arange(tokens // width, dtype=jnp.int32)[None, :] * width
    there = ((bases >= 0) & (bases <= place * tokens))[:, None, None]
    lo, hi = low_key[:, :, None], low_key[:, :, None] + width - 1
    low, high, own = tree_spans[0], tree_spans[1], tree_spans[2]
    some = ((low <= hi) & (high > lo) & (high > low)) | ((own <= hi) & (pos >= lo))
    every = ((low <= lo) & (high > hi)) | ((own <= lo) & (pos >= hi))
    per_tile = (4, tokens // KB, 2, rows // QB, QB // group)
    some = jnp.any((some & there).reshape(per_tile), axis=4)
    every = jnp.all(every.reshape(per_tile), axis=(2, 4))
    halves = some[:, :, 0] + 2 * some[:, :, 1]
    flags = jnp.where((halves == 3) & every, 4, halves).astype(jnp.int32).reshape(4, -1)
    table = jnp.concatenate([bases[:, None], flags], axis=1)

    def run(which, kv, acc, kind=jnp.bfloat16, passed=None):
        return tiles(which, table, spans, q, g, norm, delta, kv, acc, scale, kind, passed)

    *acc, part = run(0, kv_1, None)
    from_1 = back_by(part, 1)
    *acc, part = run(1, kv_2, acc)
    from_2 = back_by(part, 2)
    *acc, part, kept = run(2, kv_3, acc, passed=from_1)
    from_3 = back_by(part, 3)
    *acc, part = run(3, own_kv, acc, jnp.float32)
    dq_own, *dq_other = round_up(acc, scale)
    others = [swap(block) for block in dq_other]
    query_grad, total = gather_heads(here, dq_own, others, group, [part, kept, from_2])
    key_grad, value_grad = finish(total, from_3, scale)
    return (query_grad, key_grad, value_grad)


def solution(mesh):
    shards = mesh.shape["outer"] * mesh.shape["inner"]
    placed = (
        P(SEQ, None, "head", None),
        P(SEQ, None, None),
        P(SEQ, None, None),
        P(SEQ, None, "head", None),
        P(SEQ, None, "head", None),
        P(None, "head", SEQ),
        P(None, SEQ),
    )
    return jax.shard_map(
        functools.partial(on_device, shards),
        mesh=mesh,
        in_specs=placed,
        out_specs=(P(SEQ, None, "head", None), P(SEQ, "head", None), P(SEQ, "head", None)),
        check_vma=False,
    )
```
